32 devices in a mesh: groups: 2 (over x), row: 16 (over z, y, core).
Axes of the slice: x: 2, y: 2, z: 4, core: 2. Of those that a mesh axis runs over, the one named last changes fastest.
Arguments:
- features: bfloat16 [64, 32, 4, 256], P('groups', 'row'), parts along dimension 0, may hold values from -6 to 6
- axial_taps: float32 [31, 256], replicated, may hold values from -1 to 1
- radial_taps: float32 [31, 256], replicated, may hold values from -1 to 1
- conv_bias: float32 [256], replicated, may hold values from -6 to 6
- ln_gain: float32 [256], replicated, may hold values from 0.5 to 1.5
- ln_bias: float32 [256], replicated, may hold values from -3 to 3
- w_in: bfloat16 [1024, 256], P('row'), may hold values from -0.375 to 0.375
- b_in: bfloat16 [1024], P('row'), may hold values from -3 to 3
- w_out: bfloat16 [1024, 256], P('row'), may hold values from -0.1875 to 0.1875
- b_out: float32 [256], replicated, may hold values from -1.75 to 1.75
- layer_scale: float32 [256], replicated, may hold values from 0.5 to 2
Outputs:
- block_out: bfloat16 [64, 32, 4, 256], P('groups', 'row'), parts along dimension 0
The draws below stay inside these ranges and needn't reach their ends.
There are 2 independent parts, one for each index of `groups`. The reference program is written for one: setup_inputs(seed, part) draws one part's arguments, and reference() takes and returns one part's arrays. A program takes and returns all parts, laid end to end along the dimension named above; an argument that names none is the same for every part. Nothing has to cross between parts.
All inputs are finite; a program needn't handle non-finite values.
Results may differ from the reference program's by a relative error of at most 0.01.
Values may be sent and summed in bfloat16 or wider, within the bound.
A program may use at most 64 MiB of HBM per device.

```python
import math
from functools import partial
import jax
import jax.numpy as jnp
from jax import lax

C = 256
HID = 1024
TAPS = 31
AX_DEV = 2
THETA = 4
AXIAL = 32
RADIAL = 32


def shard_levels(key, shape, pieces, least, largest):
    loudness = 1.0
    for axis_at, parts in pieces:
        draws = jax.random.uniform(jax.random.fold_in(jax.random.fold_in(key, 6), axis_at), (parts,), jnp.float32, least / len(pieces), largest / len(pieces))
        loudness = loudness * jnp.repeat(jnp.exp(draws), shape[axis_at] // parts).reshape((-1,) + (1,) * (len(shape) - 1 - axis_at))
    return loudness


def normal_values(rng, dims, width, reach, pieces=(), dtype=jnp.bfloat16):
    level = shard_levels(rng, dims, pieces, -0.22, 0.18) if pieces else 1.0
    entries = jax.random.normal(rng, dims, jnp.float32) * width * level
    return jnp.minimum(jnp.maximum(entries, -reach), reach).astype(dtype)


def setup_inputs(seed: int = 0, part: int = 0) -> dict:
    key_of = jax.random.split(jax.random.key(seed), 12)
    part_splits = jax.random.split(jax.random.fold_in(key_of[11], part), 12)
    features = normal_values(part_splits[0], (AXIAL, RADIAL, THETA, C), 1.0, 6.0, ((1, 16),))
    axial_taps = normal_values(key_of[1], (TAPS, C), TAPS ** -0.5, 1.0, (), jnp.float32)
    radial_taps = normal_values(key_of[2], (TAPS, C), TAPS ** -0.5, 1.0, (), jnp.float32)
    conv_bias = normal_values(key_of[3], (C,), 1.0, 6.0, (), jnp.float32)
    ln_gain = jnp.clip(jax.random.uniform(key_of[4], (C,), jnp.float32, 0.5, 1.5), 0.5, 1.5)
    ln_bias = normal_values(key_of[5], (C,), 0.5, 3.0, (), jnp.float32)
    w_in = normal_values(key_of[6], (HID, C), C ** -0.5, 0.375, ((0, 16),))
    b_in = normal_values(key_of[7], (HID,), 0.5, 3.0, ((0, 16),))
    w_out = normal_values(key_of[8], (HID, C), HID ** -0.5, 0.1875, ((0, 16),))
    b_out = normal_values(key_of[9], (C,), 0.3, 1.75, (), jnp.float32)
    layer_scale = jnp.clip(jnp.exp(jax.random.uniform(key_of[10], (C,), jnp.float32, math.log(0.5), math.log(2.0))), 0.5, 2.0)
    return {"features": features, "axial_taps": axial_taps, "radial_taps": radial_taps, "conv_bias": conv_bias, "ln_gain": ln_gain, "ln_bias": ln_bias, "w_in": w_in, "b_in": b_in, "w_out": w_out, "b_out": b_out, "layer_scale": layer_scale}


def shifted_sum(source, tap_table, along_dim):
    half_span = tap_table.shape[0] // 2
    pad_widths = [(0, 0)] * source.ndim
    pad_widths[along_dim] = (half_span, half_span)
    padded = jnp.pad(source, pad_widths)
    extent = source.shape[along_dim]
    total_sum = jnp.zeros(source.shape, jnp.float32)
    for offset in range(tap_table.shape[0]):
        window = lax.slice_in_dim(padded, offset, offset + extent, axis=along_dim)
        total_sum = total_sum + window.astype(jnp.float32) * tap_table[offset]
    return total_sum

def block_mlp(params, row_block):
    w_in, b_in, w_out, ln_gain, ln_bias, b_out, layer_scale = params
    values = row_block.astype(jnp.float32)
    average = lax.optimization_barrier(jnp.mean(values, axis=-1, keepdims=True))
    centred = values - average
    variance = lax.optimization_barrier(jnp.mean(centred * centred, axis=-1, keepdims=True))
    normed = (centred * lax.rsqrt(variance + 1e-06) * ln_gain + ln_bias).astype(jnp.bfloat16)
    pre_act = lax.dot_general(normed, w_in, (((1,), (1,)), ((), ())), preferred_element_type=jnp.float32)
    pre_act = pre_act + b_in.astype(jnp.float32)
    hidden = jax.nn.gelu(pre_act, approximate=True).astype(jnp.bfloat16)
    projected = jnp.dot(hidden, w_out, preferred_element_type=jnp.float32) + b_out
    return (layer_scale * projected).astype(jnp.bfloat16)

def reference(features, axial_taps, radial_taps, conv_bias, ln_gain, ln_bias, w_in, b_in, w_out, b_out, layer_scale):
    params = (w_in, b_in, w_out, ln_gain, ln_bias, b_out, layer_scale)
    planes = jnp.moveaxis(features, 2, 0)
    channels = features.shape[-1]

    def one_plane(theta_plane):
        axial_mixed = shifted_sum(theta_plane, axial_taps, 0).astype(jnp.bfloat16)
        radial_mixed = (shifted_sum(axial_mixed, radial_taps, 1) + conv_bias).astype(jnp.bfloat16)
        groups = radial_mixed.reshape(AXIAL // AX_DEV, AX_DEV * RADIAL, channels)
        branch = lax.map(partial(block_mlp, params), groups).reshape(AXIAL, RADIAL, channels)
        return (theta_plane.astype(jnp.float32) + branch.astype(jnp.float32)).astype(jnp.bfloat16)
    result = lax.map(one_plane, planes)
    return jnp.moveaxis(result, 0, 2)
```

```python
import functools

import jax
import jax.numpy as jnp
from jax import lax
from jax.experimental import pallas as pl
from jax.experimental.pallas import tpu as pltpu
from jax.sharding import PartitionSpec as P

MESH_ID = pl.DeviceIdType.MESH
F32 = jnp.float32
BF16 = jnp.bfloat16


def swap_middle(first, second):
    top = lax.broadcasted_iota(jnp.int32, first.shape, first.ndim - 2) < 4
    axis = first.ndim - 2
    return (
        jnp.where(top, first, pltpu.roll(second, 4, axis)),
        jnp.where(top, pltpu.roll(first, 4, axis), second),
    )


def kernel(
    n, inner, taps, hl,
    x_ref, at_ref, rt_ref, cb_ref, lg_ref, lb_ref, wi_ref, bi_ref, wo_ref, bo_ref, ls_ref,
    o_ref,
    xb, atv, rtv, cbv, lgv, lbv, biv, bov, lsv,
    xpad, rpad, send1, recv1, send2, recv2, wts, bias,
    in_sem, up_sem, across_sem, s1_sem, r1_sem, s2_sem, r2_sem, ws_sem, wr_sem, bs_sem, br_sem,
):
    channels = x_ref.shape[3]
    axial = x_ref.shape[0]
    half = taps // 2
    per = channels // hl
    chips = n // 2
    outer = chips // inner
    q = 2 * inner
    me = lax.axis_index("row")
    grp = lax.axis_index("groups")
    core = lax.rem(me, 2)
    my_chip = lax.div(me, 2)
    my_z = lax.div(my_chip, inner)
    my_y = lax.rem(my_chip, inner)
    sibling = me + 1 - 2 * core
    base = core * chips
    my_slot = base + my_chip
    last = outer - 1
    mine = grp * n
    theirs = (1 - grp) * n

    def to(d):
        return (grp, d)

    def loop(lo, hi, body):
        def step(i, c):
            body(i)
            return c

        lax.fori_loop(lo, hi, step, 0)

    barrier = pltpu.get_barrier_semaphore()
    loop(me + 1, n, lambda d: pl.semaphore_signal(barrier, inc=1, device_id=to(d), device_id_type=MESH_ID))

    @pl.when(grp == 0)
    def _():
        pl.semaphore_signal(barrier, inc=1, device_id=(1, me), device_id_type=MESH_ID)

    pairs = (
        (wi_ref, wts.at[my_slot]), (wo_ref, wts.at[n + my_slot]), (bi_ref, biv), (x_ref, xb), (at_ref, atv), (rt_ref, rtv),
        (cb_ref, cbv), (lg_ref, lgv), (lb_ref, lbv), (bo_ref, bov), (ls_ref, lsv),
    )
    loads = [pltpu.make_async_copy(a, b, in_sem.at[i]) for i, (a, b) in enumerate(pairs)]
    for copy in loads:
        copy.start()

    @pl.when(me + grp > 0)
    def _():
        pl.semaphore_wait(barrier, me + grp)

    @pl.when(grp == 1)
    def _():
        pl.semaphore_signal(across_sem, inc=1, device_id=(0, me), device_id_type=MESH_ID)

    loop(0, me, lambda d: pl.semaphore_signal(up_sem.at[my_z], inc=1, device_id=to(d), device_id_type=MESH_ID))

    for copy in loads[:3]:
        copy.wait()
    unit = lax.broadcasted_iota(jnp.int32, (hl, channels), 0)
    lane = lax.broadcasted_iota(jnp.int32, (hl, channels), 1)
    place = (lane == unit + lax.rem(my_slot, per) * hl).astype(F32).astype(BF16)
    bias16 = jnp.broadcast_to(biv[...].astype(F32), (16, hl)).astype(BF16)
    bias[my_slot] = jnp.dot(bias16, place, preferred_element_type=F32)[0:1]

    def piece_copy(piece, g, d):
        return pltpu.make_async_remote_copy(
            src_ref=wts.at[piece], dst_ref=wts.at[piece], send_sem=ws_sem, recv_sem=wr_sem.at[piece],
            device_id=(g, d), device_id_type=MESH_ID,
        )

    def device(z, y):
        return 2 * (z * inner + y) + core

    def to_plane(z):
        @pl.when(my_z == last)
        def _():
            loop(0, inner, lambda j: piece_copy(mine + my_slot, grp, device(z, lax.rem(my_y + j, inner))).start())

        @pl.when(my_z != last)
        def _():
            piece_copy(mine + my_slot, grp, device(z, my_y)).start()

    def to_inner(piece):
        loop(1, inner, lambda j: piece_copy(piece, grp, device(my_z, lax.rem(my_y + j, inner))).start())

    @pl.when(my_z > 0)
    def _():
        to_plane(0)

    loads[3].wait()
    loads[4].wait()
    xpad[0:half] = jnp.zeros((half, 8, channels), F32)
    xpad[axial + half : axial + 2 * half] = jnp.zeros((half, 8, channels), F32)

    def widen(i):
        for j in range(8):
            for r in range(2):
                xpad[half + i * 8 + j, 4 * r : 4 * r + 4, :] = xb[i * 8 + j, r].astype(F32)

    loop(0, axial // 8, widen)

    def axial_chunk(i):
        acc = jnp.zeros((8, 8, channels), F32)
        for k in range(taps):
            acc = acc + xpad[pl.ds(i * 8 + k, 8)] * atv[k : k + 1, :][None]
        acc = acc.reshape(4, 2, 8, channels)
        low, high = swap_middle(acc[:, 0], acc[:, 1])
        send1[pl.ds(i * 4, 4)] = jnp.concatenate([low, high], axis=1).astype(BF16)

    loop(0, axial // 8, axial_chunk)

    def exchange1(d):
        pltpu.make_async_remote_copy(
            src_ref=send1.at[d], dst_ref=recv1.at[me], send_sem=s1_sem, recv_sem=r1_sem.at[my_z],
            device_id=to(d), device_id_type=MESH_ID,
        ).start()

    def send_bias(d):
        pltpu.make_async_remote_copy(
            src_ref=bias.at[my_slot], dst_ref=bias.at[my_slot], send_sem=bs_sem, recv_sem=br_sem,
            device_id=to(d), device_id_type=MESH_ID,
        ).start()

    loop(0, me, exchange1)
    pltpu.make_async_copy(send1.at[me], recv1.at[me], r1_sem.at[my_z]).start()
    loop(1, my_z, to_plane)
    loop(0, me, send_bias)

    def upward(z):
        behind = jnp.where(z == my_z, lax.rem(me, q), -1)

        @pl.when(behind < q - 1)
        def _():
            pl.semaphore_wait(up_sem.at[z], q - 1 - behind)

        loop(z * q + behind + 1, z * q + q, exchange1)

        @pl.when(z == my_z)
        def _():
            to_inner(mine + my_slot)
            piece_copy(mine + my_slot, grp, sibling).start()
            piece_copy(theirs + my_slot, grp, sibling).start()

        @pl.when(z != my_z)
        def _():
            to_plane(z)

        loop(z * q + behind + 1, z * q + q, send_bias)

    loop(my_z, outer, upward)

    @pl.when(grp == 0)
    def _():
        pl.semaphore_wait(across_sem, 1)

    def pass_on(piece):
        piece_copy(piece, 1 - grp, me).start()
        piece_copy(piece, grp, sibling).start()

    def from_line(z):
        piece = mine + base + z * inner + my_y
        piece_copy(piece, grp, sibling).wait_recv()

        @pl.when(z != last)
        def _():
            to_inner(piece)

        pass_on(piece)

    def from_inner(z):
        def step(j):
            piece = mine + base + z * inner + lax.rem(my_y + j, inner)
            piece_copy(piece, grp, sibling).wait_recv()
            pass_on(piece)

        loop(1, inner, step)

    def from_across(z):
        piece = theirs + base + z
        piece_copy(piece, grp, sibling).wait_recv()
        piece_copy(piece, grp, sibling).start()

    inside = my_z < last
    near = jnp.where(inside, my_z, 0)
    from_inner(my_z)
    loop(0, near, from_line)
    loop(my_z + 1, jnp.where(my_z == 0, outer, last), from_line)

    rpad[0:half] = jnp.zeros((half, 8, channels), F32)
    rpad[2 * n + half : 2 * n + 2 * half] = jnp.zeros((half, 8, channels), F32)
    loads[5].wait()
    loads[6].wait()

    def take(z):
        plane = recv1.at[pl.ds(z * q, q)]
        pltpu.make_async_copy(plane, plane, r1_sem.at[z]).wait()
        v = recv1[z * q : z * q + q].astype(F32)
        rpad[half + 2 * z * q : half + 2 * z * q + 2 * q] = v.reshape(2 * q, 8, channels)

    my_half = lax.div(me, n // 2)

    def exchange2(d):
        @pl.when(d != me)
        def _():
            pltpu.make_async_remote_copy(
                src_ref=send2.at[d], dst_ref=recv2.at[me], send_sem=s2_sem, recv_sem=r2_sem.at[my_half],
                device_id=to(d), device_id_type=MESH_ID,
            ).start()

        @pl.when(d == me)
        def _():
            pltpu.make_async_copy(send2.at[me], recv2.at[me], r2_sem.at[my_half]).start()

    def radial_chunk(i):
        acc = jnp.zeros((8, 8, channels), F32)
        for k in range(taps):
            acc = acc + rpad[pl.ds(i * 8 + k, 8)] * rtv[k : k + 1, :][None]
        acc = acc + cbv[...][None]
        send2[pl.ds(i * 4, 4)] = acc.reshape(4, 16, channels).astype(BF16)
        loop(i * 4, i * 4 + 4, exchange2)

    taken = 0
    for z in range(outer):
        need = min(outer, (q * z + q - 1 + 8) // q + 1)
        for p in range(taken, need):
            take(p)
        taken = need
        loop(z * q // 4, (z + 1) * q // 4, radial_chunk)

    loop(0, jnp.where(inside, 0, last), from_line)
    loop(jnp.where(inside & (my_z > 0), last, outer), outer, from_line)
    loop(jnp.where(inside, last, outer), outer, from_inner)
    loop(0, my_z, from_inner)
    loop(my_z + 1, last, from_inner)
    loop(1, chips, lambda i: from_across(lax.rem(my_chip + i, chips)))

    def from_sibling(i):
        piece_copy((1 - core) * chips + i, grp, sibling).wait_recv()
        piece_copy(n + (1 - core) * chips + i, grp, sibling).wait_recv()

    biases = bias.at[pl.ds(0, n - 1)]
    pltpu.make_async_copy(biases, biases, br_sem).wait()
    loop(0, chips, from_sibling)
    for copy in loads[7:]:
        copy.wait()

    block = min(8, n // 2)
    rows = block * 16

    def flat(w):
        if hl % 16:
            return w.astype(F32).reshape(per * hl, channels).astype(BF16)
        return w.reshape(per * hl, channels)

    def project(z, first):
        w_in = flat(wts[pl.ds(first, per)])
        w_out = flat(wts[pl.ds(n + first, per)])
        b_in = jnp.sum(bias[pl.ds(first, per)], axis=0)
        u = lax.dot_general(z, w_in, (((1,), (1,)), ((), ())), preferred_element_type=F32) + b_in
        g = 0.5 * u * (1.0 + jnp.tanh(0.7978845608028654 * (u + 0.044715 * (u * u * u))))
        return jnp.dot(g.astype(BF16), w_out, preferred_element_type=F32)

    def mlp(first):
        v = recv2[pl.ds(first, block)].reshape(rows, channels).astype(F32)
        average = jnp.mean(v, axis=-1, keepdims=True)
        centred = v - average
        variance = jnp.mean(centred * centred, axis=-1, keepdims=True)
        z = (centred * lax.rsqrt(variance + 1e-06) * lgv[...] + lbv[...]).astype(BF16)
        total = project(z, 0)
        for g in range(1, n // per):
            total = total + project(z, g * per)
        branch = (lsv[...] * (total + bov[...])).astype(BF16).astype(F32)
        branch = branch.reshape(block, 2, 8, channels)
        for a, part in enumerate(swap_middle(branch[:, 0], branch[:, 1])):
            for s in range(block):
                at = 2 * (first + s) + a
                v = xpad[half + at] + part[s]
                for r in range(2):
                    o_ref[at, r] = v[4 * r : 4 * r + 4].astype(BF16)

    upper = lax.div(my_z, (outer + 1) // 2)
    for b in range(2):
        h = jnp.where(upper == 0, b, 1 - b)
        part = recv2.at[pl.ds(0, n // 2)]
        pltpu.make_async_copy(part, part, r2_sem.at[h]).wait()
        loop(0, n // 2 // block, lambda i: mlp(h * (n // 2) + i * block))

    sent = send1.at[pl.ds(0, n - 1)]
    pltpu.make_async_copy(sent, sent, s1_sem).wait()
    sent2 = send2.at[pl.ds(0, n - 1)]
    pltpu.make_async_copy(sent2, sent2, s2_sem).wait()
    passed = wts.at[pl.ds(0, 2 * n - 1 - inner)]
    pltpu.make_async_copy(passed, passed, ws_sem).wait()

    @pl.when(my_z == last)
    def _():
        more = wts.at[pl.ds(0, outer * (inner - 1))]
        pltpu.make_async_copy(more, more, ws_sem).wait()

    pltpu.make_async_copy(biases, biases, bs_sem).wait()


def local(
    features,
    axial_taps,
    radial_taps,
    conv_bias,
    ln_gain,
    ln_bias,
    w_in,
    b_in,
    w_out,
    b_out,
    layer_scale,
    n,
    groups,
):
    axial, radial, theta, channels = features.shape
    taps = axial_taps.shape[0]
    hl = w_in.shape[0]
    inner = 1
    while 4 * inner * inner <= n // 2:
        inner *= 2
    assert groups == 2
    assert radial == 2 and theta == 4 and axial == 2 * n and channels == 256 and taps == 31

    def row(v):
        return v.reshape(1, -1)

    vmem = pl.BlockSpec(memory_space=pltpu.VMEM)
    hbm = pl.BlockSpec(memory_space=pltpu.HBM)
    dma = pltpu.SemaphoreType.DMA
    vec = pltpu.VMEM((1, channels), F32)
    return pl.pallas_call(
        functools.partial(kernel, n, inner, taps, hl),
        out_shape=pltpu.VMEM(features.shape, BF16),
        in_specs=[hbm] * 11,
        out_specs=vmem,
        scratch_shapes=[
            pltpu.VMEM(features.shape, BF16),
            pltpu.VMEM((taps, channels), F32),
            pltpu.VMEM((taps, channels), F32),
            vec, vec, vec,
            pltpu.VMEM((1, hl), BF16),
            vec, vec,
            pltpu.VMEM((axial + taps - 1, 8, channels), F32),
            pltpu.VMEM((2 * n + taps - 1, 8, channels), F32),
            pltpu.VMEM((n, 16, channels), BF16),
            pltpu.VMEM((n, 16, channels), BF16),
            pltpu.VMEM((n, 16, channels), BF16),
            pltpu.VMEM((n, 16, channels), BF16),
            pltpu.VMEM((2 * n, hl, channels), BF16),
            pltpu.VMEM((n, 1, channels), F32),
            dma((11,)),
            pltpu.SemaphoreType.REGULAR((n // 2 // inner,)),
            pltpu.SemaphoreType.REGULAR,
            dma, dma((n // 2 // inner,)), dma, dma((2,)), dma,
            dma((2 * n,)), dma, dma,
        ],
        compiler_params=pltpu.CompilerParams(
            collective_id=0, has_side_effects=True, vmem_limit_bytes=60 * 1024 * 1024
        ),
        cost_estimate=pl.CostEstimate(
            flops=axial * 8 * channels * 4 * (n * hl + taps),
            bytes_accessed=4 * axial * 8 * channels + 4 * n * hl * channels,
            transcendentals=axial * 8 * n * hl,
        ),
    )(
        features, axial_taps, radial_taps, row(conv_bias), row(ln_gain), row(ln_bias),
        w_in, row(b_in), w_out, row(b_out), row(layer_scale),
    )


def solution(mesh):
    in_specs = (
        P("groups", "row", None, None),
        P(),
        P(),
        P(),
        P(),
        P(),
        P("row", None),
        P("row"),
        P("row", None),
        P(),
        P(),
    )
    out_specs = P("groups", "row", None, None)
    body = functools.partial(local, n=mesh.shape["row"], groups=mesh.shape["groups"])
    return jax.shard_map(body, mesh=mesh, in_specs=in_specs, out_specs=out_specs, check_vma=False)
```

```python
import functools

import jax
import jax.numpy as jnp
from jax import lax
from jax.experimental import pallas as pl
from jax.experimental.pallas import tpu as pltpu
from jax.sharding import PartitionSpec as P

MESH_ID = pl.DeviceIdType.MESH
F32 = jnp.float32
BF16 = jnp.bfloat16


def swap_middle(first, second):
    top = lax.broadcasted_iota(jnp.int32, first.shape, first.ndim - 2) < 4
    axis = first.ndim - 2
    return (
        jnp.where(top, first, pltpu.roll(second, 4, axis)),
        jnp.where(top, pltpu.roll(first, 4, axis), second),
    )


def kernel(
    n, inner, taps, hl,
    x_ref, at_ref, rt_ref, cb_ref, lg_ref, lb_ref, wi_ref, bi_ref, wo_ref, bo_ref, ls_ref,
    o_ref,
    xb, atv, rtv, cbv, lgv, lbv, biv, bov, lsv,
    xpad, rpad, send1, recv1, send2, recv2, wts, bias, normed, sums,
    in_sem, up_sem, across_sem, s1_sem, r1_sem, s2_sem, r2_sem, ws_sem, wr_sem, bs_sem, br_sem,
):
    channels = x_ref.shape[3]
    axial = x_ref.shape[0]
    half = taps // 2
    per = channels // hl
    chips = n // 2
    outer = chips // inner
    q = 2 * inner
    me = lax.axis_index("row")
    grp = lax.axis_index("groups")
    core = lax.rem(me, 2)
    my_chip = lax.div(me, 2)
    my_z = lax.div(my_chip, inner)
    my_y = lax.rem(my_chip, inner)
    sibling = me + 1 - 2 * core
    base = core * chips
    my_slot = base + my_chip
    last = outer - 1
    mine = grp * n
    theirs = (1 - grp) * n

    def to(d):
        return (grp, d)

    def loop(lo, hi, body):
        def step(i, c):
            body(i)
            return c

        lax.fori_loop(lo, hi, step, 0)

    barrier = pltpu.get_barrier_semaphore()
    loop(me + 1, n, lambda d: pl.semaphore_signal(barrier, inc=1, device_id=to(d), device_id_type=MESH_ID))

    @pl.when(grp == 0)
    def _():
        pl.semaphore_signal(barrier, inc=1, device_id=(1, me), device_id_type=MESH_ID)

    pairs = (
        (wi_ref, wts.at[my_slot]), (wo_ref, wts.at[n + my_slot]), (bi_ref, biv), (x_ref, xb), (at_ref, atv), (rt_ref, rtv),
        (cb_ref, cbv), (lg_ref, lgv), (lb_ref, lbv), (bo_ref, bov), (ls_ref, lsv),
    )
    loads = [pltpu.make_async_copy(a, b, in_sem.at[i]) for i, (a, b) in enumerate(pairs)]
    for copy in loads:
        copy.start()

    @pl.when(me + grp > 0)
    def _():
        pl.semaphore_wait(barrier, me + grp)

    @pl.when(grp == 1)
    def _():
        pl.semaphore_signal(across_sem, inc=1, device_id=(0, me), device_id_type=MESH_ID)

    loop(0, me, lambda d: pl.semaphore_signal(up_sem.at[my_z], inc=1, device_id=to(d), device_id_type=MESH_ID))

    for copy in loads[:3]:
        copy.wait()
    unit = lax.broadcasted_iota(jnp.int32, (hl, channels), 0)
    lane = lax.broadcasted_iota(jnp.int32, (hl, channels), 1)
    place = (lane == unit + lax.rem(my_slot, per) * hl).astype(F32).astype(BF16)
    bias16 = jnp.broadcast_to(biv[...].astype(F32), (16, hl)).astype(BF16)
    bias[my_slot] = jnp.dot(bias16, place, preferred_element_type=F32)[0:1]

    def piece_copy(piece, g, d):
        return pltpu.make_async_remote_copy(
            src_ref=wts.at[piece], dst_ref=wts.at[piece], send_sem=ws_sem, recv_sem=wr_sem.at[piece],
            device_id=(g, d), device_id_type=MESH_ID,
        )

    def device(z, y):
        return 2 * (z * inner + y) + core

    def to_plane(z):
        @pl.when(my_z == last)
        def _():
            loop(0, inner, lambda j: piece_copy(mine + my_slot, grp, device(z, lax.rem(my_y + j, inner))).start())

        @pl.when(my_z != last)
        def _():
            piece_copy(mine + my_slot, grp, device(z, my_y)).start()

    def to_inner(piece):
        loop(1, inner, lambda j: piece_copy(piece, grp, device(my_z, lax.rem(my_y + j, inner))).start())

    @pl.when(my_z > 0)
    def _():
        to_plane(0)

    loads[3].wait()
    loads[4].wait()
    xpad[0:half] = jnp.zeros((half, 8, channels), F32)
    xpad[axial + half : axial + 2 * half] = jnp.zeros((half, 8, channels), F32)

    def widen(i):
        for j in range(8):
            for r in range(2):
                xpad[half + i * 8 + j, 4 * r : 4 * r + 4, :] = xb[i * 8 + j, r].astype(F32)

    loop(0, axial // 8, widen)

    def axial_chunk(i):
        acc = jnp.zeros((8, 8, channels), F32)
        for k in range(taps):
            acc = acc + xpad[pl.ds(i * 8 + k, 8)] * atv[k : k + 1, :][None]
        acc = acc.reshape(4, 2, 8, channels)
        low, high = swap_middle(acc[:, 0], acc[:, 1])
        send1[pl.ds(i * 4, 4)] = jnp.concatenate([low, high], axis=1).astype(BF16)

    loop(0, axial // 8, axial_chunk)

    def exchange1(d):
        pltpu.make_async_remote_copy(
            src_ref=send1.at[d], dst_ref=recv1.at[me], send_sem=s1_sem, recv_sem=r1_sem.at[my_z],
            device_id=to(d), device_id_type=MESH_ID,
        ).start()

    def send_bias(d):
        pltpu.make_async_remote_copy(
            src_ref=bias.at[my_slot], dst_ref=bias.at[my_slot], send_sem=bs_sem, recv_sem=br_sem,
            device_id=to(d), device_id_type=MESH_ID,
        ).start()

    loop(0, me, exchange1)
    pltpu.make_async_copy(send1.at[me], recv1.at[me], r1_sem.at[my_z]).start()
    loop(1, my_z, to_plane)
    loop(0, me, send_bias)

    def upward(z):
        behind = jnp.where(z == my_z, lax.rem(me, q), -1)

        @pl.when(behind < q - 1)
        def _():
            pl.semaphore_wait(up_sem.at[z], q - 1 - behind)

        loop(z * q + behind + 1, z * q + q, exchange1)

        @pl.when(z == my_z)
        def _():
            to_inner(mine + my_slot)
            pl.when(core == 1)(lambda: to_inner(theirs + my_slot))
            piece_copy(mine + my_slot, grp, sibling).start()
            piece_copy(theirs + my_slot, grp, sibling).start()

        @pl.when(z != my_z)
        def _():
            to_plane(z)

        loop(z * q + behind + 1, z * q + q, send_bias)

    loop(my_z, outer, upward)

    @pl.when(grp == 0)
    def _():
        pl.semaphore_wait(across_sem, 1)

    def pass_on(piece):
        piece_copy(piece, 1 - grp, me).start()
        piece_copy(piece, grp, sibling).start()

    def from_line(z):
        piece = mine + base + z * inner + my_y
        piece_copy(piece, grp, sibling).wait_recv()

        @pl.when(z != last)
        def _():
            to_inner(piece)

        pass_on(piece)

    def from_inner(z):
        def step(j):
            piece = mine + base + z * inner + lax.rem(my_y + j, inner)
            piece_copy(piece, grp, sibling).wait_recv()

            @pl.when((core == 0) | ((z == last) & inside))
            def _():
                piece_copy(piece, 1 - grp, me).start()

            piece_copy(piece, grp, sibling).start()

        loop(1, inner, step)

    def from_across(z, y):
        piece = theirs + base + z * inner + y
        piece_copy(piece, grp, sibling).wait_recv()

        @pl.when((core == 1) & (y == my_y) & (z != last))
        def _():
            to_inner(piece)

        piece_copy(piece, grp, sibling).start()

    inside = my_z < last

    def nearest(visit):
        def step(dist):
            for z in (my_z - dist, my_z + dist):

                @pl.when((z >= 0) & (z < outer))
                def _(z=z):
                    visit(z)

        loop(1, outer, step)

    def early(z):
        return (inside & ((z < last) | (my_z == 0))) | ((my_z == last) & (z == last - 1))

    @pl.when(inside)
    def _():
        from_inner(my_z)

    nearest(lambda z: pl.when(early(z))(lambda: from_line(z)))

    rpad[0:half] = jnp.zeros((half, 8, channels), F32)
    rpad[2 * n + half : 2 * n + 2 * half] = jnp.zeros((half, 8, channels), F32)
    loads[5].wait()
    loads[6].wait()

    def take(z):
        plane = recv1.at[pl.ds(z * q, q)]
        pltpu.make_async_copy(plane, plane, r1_sem.at[z]).wait()
        v = recv1[z * q : z * q + q].astype(F32)
        rpad[half + 2 * z * q : half + 2 * z * q + 2 * q] = v.reshape(2 * q, 8, channels)

    my_half = lax.div(me, n // 2)

    def exchange2(d):
        @pl.when(d != me)
        def _():
            pltpu.make_async_remote_copy(
                src_ref=send2.at[d], dst_ref=recv2.at[me], send_sem=s2_sem, recv_sem=r2_sem.at[my_half],
                device_id=to(d), device_id_type=MESH_ID,
            ).start()

        @pl.when(d == me)
        def _():
            pltpu.make_async_copy(send2.at[me], recv2.at[me], r2_sem.at[my_half]).start()

    def radial_chunk(i):
        acc = jnp.zeros((8, 8, channels), F32)
        for k in range(taps):
            acc = acc + rpad[pl.ds(i * 8 + k, 8)] * rtv[k : k + 1, :][None]
        acc = acc + cbv[...][None]
        send2[pl.ds(i * 4, 4)] = acc.reshape(4, 16, channels).astype(BF16)
        loop(i * 4, i * 4 + 4, exchange2)

    taken = 0
    for z in range(outer):
        need = min(outer, (q * z + q - 1 + 8) // q + 1)
        for p in range(taken, need):
            take(p)
        taken = need
        loop(z * q // 4, (z + 1) * q // 4, radial_chunk)


    @pl.when(my_z == last)
    def _():
        from_inner(my_z)

    nearest(lambda z: pl.when(jnp.logical_not(early(z)))(lambda: from_line(z)))
    nearest(from_inner)

    def across_inner(j):
        y = lax.rem(my_y + j, inner)

        @pl.when(j > 0)
        def _():
            from_across(my_z, y)

        nearest(lambda z: from_across(z, y))

    loop(0, inner, across_inner)

    biases = bias.at[pl.ds(0, n - 1)]
    pltpu.make_async_copy(biases, biases, br_sem).wait()
    for copy in loads[7:]:
        copy.wait()
    block = min(16, n)
    rows = block * 16

    def norm(i):
        v = recv2[pl.ds(i * block, block)].reshape(rows, channels).astype(F32)
        average = jnp.mean(v, axis=-1, keepdims=True)
        centred = v - average
        variance = jnp.mean(centred * centred, axis=-1, keepdims=True)
        z = centred * lax.rsqrt(variance + 1e-06) * lgv[...] + lbv[...]
        normed[i] = z.astype(BF16)

    for h in range(2):
        part = recv2.at[pl.ds(0, n // 2)]
        pltpu.make_async_copy(part, part, r2_sem.at[h]).wait()
    loop(0, n // block, norm)

    def flat(w):
        if hl % 16:
            return w.astype(F32).reshape(per * hl, channels).astype(BF16)
        return w.reshape(per * hl, channels)

    def project(z, first):
        w_in = flat(wts[pl.ds(first, per)])
        w_out = flat(wts[pl.ds(n + first, per)])
        b_in = jnp.sum(bias[pl.ds(first, per)], axis=0)
        u = lax.dot_general(z, w_in, (((1,), (1,)), ((), ())), preferred_element_type=F32) + b_in
        g = 0.5 * u * (1.0 + jnp.tanh(0.7978845608028654 * (u + 0.044715 * (u * u * u))))
        return jnp.dot(g.astype(BF16), w_out, preferred_element_type=F32)

    def from_sibling(i):
        piece_copy(i, grp, sibling).wait_recv()
        piece_copy(n + i, grp, sibling).wait_recv()

    def half_mlp(first):
        def step(i):
            total = project(normed[i], first)
            for g in range(1, chips // per):
                total = total + project(normed[i], first + g * per)
            return total

        return step

    def own(i):
        sums[i] = half_mlp(base)(i)

    loop(0, n // block, own)
    loop(chips - base, n - base, from_sibling)

    def finish(i):
        total = sums[i] + half_mlp(chips - base)(i)
        branch = (lsv[...] * (total + bov[...])).astype(BF16).astype(F32)
        branch = branch.reshape(block, 2, 8, channels)
        for a, part in enumerate(swap_middle(branch[:, 0], branch[:, 1])):
            for s in range(block):
                at = 2 * (i * block + s) + a
                v = xpad[half + at] + part[s]
                for r in range(2):
                    o_ref[at, r] = v[4 * r : 4 * r + 4].astype(BF16)

    loop(0, n // block, finish)

    sent = send1.at[pl.ds(0, n - 1)]
    pltpu.make_async_copy(sent, sent, s1_sem).wait()
    sent2 = send2.at[pl.ds(0, n - 1)]
    pltpu.make_async_copy(sent2, sent2, s2_sem).wait()
    passed = wts.at[pl.ds(0, 2 * n - 1 - inner)]
    pltpu.make_async_copy(passed, passed, ws_sem).wait()

    @pl.when(my_z == last)
    def _():
        more = wts.at[pl.ds(0, outer * (inner - 1))]
        pltpu.make_async_copy(more, more, ws_sem).wait()

    pltpu.make_async_copy(biases, biases, bs_sem).wait()


def local(
    features,
    axial_taps,
    radial_taps,
    conv_bias,
    ln_gain,
    ln_bias,
    w_in,
    b_in,
    w_out,
    b_out,
    layer_scale,
    n,
    groups,
):
    axial, radial, theta, channels = features.shape
    taps = axial_taps.shape[0]
    hl = w_in.shape[0]
    inner = 1
    while 4 * inner * inner <= n // 2:
        inner *= 2
    assert groups == 2
    assert radial == 2 and theta == 4 and axial == 2 * n and channels == 256 and taps == 31

    def row(v):
        return v.reshape(1, -1)

    vmem = pl.BlockSpec(memory_space=pltpu.VMEM)
    hbm = pl.BlockSpec(memory_space=pltpu.HBM)
    dma = pltpu.SemaphoreType.DMA
    vec = pltpu.VMEM((1, channels), F32)
    return pl.pallas_call(
        functools.partial(kernel, n, inner, taps, hl),
        out_shape=pltpu.VMEM(features.shape, BF16),
        in_specs=[hbm] * 11,
        out_specs=vmem,
        scratch_shapes=[
            pltpu.VMEM(features.shape, BF16),
            pltpu.VMEM((taps, channels), F32),
            pltpu.VMEM((taps, channels), F32),
            vec, vec, vec,
            pltpu.VMEM((1, hl), BF16),
            vec, vec,
            pltpu.VMEM((axial + taps - 1, 8, channels), F32),
            pltpu.VMEM((2 * n + taps - 1, 8, channels), F32),
            pltpu.VMEM((n, 16, channels), BF16),
            pltpu.VMEM((n, 16, channels), BF16),
            pltpu.VMEM((n, 16, channels), BF16),
            pltpu.VMEM((n, 16, channels), BF16),
            pltpu.VMEM((2 * n, hl, channels), BF16),
            pltpu.VMEM((n, 1, channels), F32),
            pltpu.VMEM((n // min(16, n), 16 * min(16, n), channels), BF16),
            pltpu.VMEM((n // min(16, n), 16 * min(16, n), channels), F32),
            dma((11,)),
            pltpu.SemaphoreType.REGULAR((n // 2 // inner,)),
            pltpu.SemaphoreType.REGULAR,
            dma, dma((n // 2 // inner,)), dma, dma((2,)), dma,
            dma((2 * n,)), dma, dma,
        ],
        compiler_params=pltpu.CompilerParams(
            collective_id=0, has_side_effects=True, vmem_limit_bytes=60 * 1024 * 1024
        ),
        cost_estimate=pl.CostEstimate(
            flops=axial * 8 * channels * 4 * (n * hl + taps),
            bytes_accessed=4 * axial * 8 * channels + 4 * n * hl * channels,
            transcendentals=axial * 8 * n * hl,
        ),
    )(
        features, axial_taps, radial_taps, row(conv_bias), row(ln_gain), row(ln_bias),
        w_in, row(b_in), w_out, row(b_out), row(layer_scale),
    )


def solution(mesh):
    in_specs = (
        P("groups", "row", None, None),
        P(),
        P(),
        P(),
        P(),
        P(),
        P("row", None),
        P("row"),
        P("row", None),
        P(),
        P(),
    )
    out_specs = P("groups", "row", None, None)
    body = functools.partial(local, n=mesh.shape["row"], groups=mesh.shape["groups"])
    return jax.shard_map(body, mesh=mesh, in_specs=in_specs, out_specs=out_specs, check_vma=False)
```

```python
import functools

import jax
import jax.numpy as jnp
from jax import lax
from jax.experimental import pallas as pl
from jax.experimental.pallas import tpu as pltpu
from jax.sharding import PartitionSpec as P

MESH_ID = pl.DeviceIdType.MESH
F32 = jnp.float32
BF16 = jnp.bfloat16


def swap_middle(first, second):
    top = lax.broadcasted_iota(jnp.int32, first.shape, first.ndim - 2) < 4
    axis = first.ndim - 2
    return (
        jnp.where(top, first, pltpu.roll(second, 4, axis)),
        jnp.where(top, pltpu.roll(first, 4, axis), second),
    )


def kernel(
    n, inner, taps, hl,
    x_ref, at_ref, rt_ref, cb_ref, lg_ref, lb_ref, wi_ref, bi_ref, wo_ref, bo_ref, ls_ref,
    o_ref,
    xb, atv, rtv, cbv, lgv, lbv, biv, bov, lsv,
    xpad, rpad, send1, recv1, send2, recv2, wts, bias, normed, sums,
    in_sem, up_sem, across_sem, s1_sem, r1_sem, s2_sem, r2_sem, ws_sem, wr_sem, bs_sem, br_sem,
):
    channels = x_ref.shape[3]
    axial = x_ref.shape[0]
    half = taps // 2
    per = channels // hl
    chips = n // 2
    outer = chips // inner
    q = 2 * inner
    me = lax.axis_index("row")
    grp = lax.axis_index("groups")
    core = lax.rem(me, 2)
    my_chip = lax.div(me, 2)
    my_z = lax.div(my_chip, inner)
    my_y = lax.rem(my_chip, inner)
    sibling = me + 1 - 2 * core
    base = core * chips
    my_slot = base + my_chip
    last = outer - 1
    inside = my_z < last
    mine = grp * n
    theirs = (1 - grp) * n

    def to(d):
        return (grp, d)

    def loop(lo, hi, body):
        def step(i, c):
            body(i)
            return c

        lax.fori_loop(lo, hi, step, 0)

    barrier = pltpu.get_barrier_semaphore()
    loop(me + 1, n, lambda d: pl.semaphore_signal(barrier, inc=1, device_id=to(d), device_id_type=MESH_ID))

    @pl.when(grp == 0)
    def _():
        pl.semaphore_signal(barrier, inc=1, device_id=(1, me), device_id_type=MESH_ID)

    pairs = (
        (x_ref, xb), (at_ref, atv), (wi_ref, wts.at[my_slot]), (wo_ref, wts.at[n + my_slot]), (bi_ref, biv),
        (rt_ref, rtv), (cb_ref, cbv), (lg_ref, lgv), (lb_ref, lbv), (bo_ref, bov), (ls_ref, lsv),
    )
    loads = [pltpu.make_async_copy(a, b, in_sem.at[i]) for i, (a, b) in enumerate(pairs)]
    for copy in loads:
        copy.start()

    @pl.when(me + grp > 0)
    def _():
        pl.semaphore_wait(barrier, me + grp)

    @pl.when(grp == 1)
    def _():
        pl.semaphore_signal(across_sem, inc=1, device_id=(0, me), device_id_type=MESH_ID)

    loop(0, me, lambda d: pl.semaphore_signal(up_sem.at[my_z], inc=1, device_id=to(d), device_id_type=MESH_ID))

    def piece_copy(piece, g, d):
        return pltpu.make_async_remote_copy(
            src_ref=wts.at[piece], dst_ref=wts.at[piece], send_sem=ws_sem, recv_sem=wr_sem.at[piece],
            device_id=(g, d), device_id_type=MESH_ID,
        )

    def device(z, y):
        return 2 * (z * inner + y) + core

    def to_plane(z):
        @pl.when(my_z == last)
        def _():
            loop(0, inner, lambda j: piece_copy(mine + my_slot, grp, device(z, lax.rem(my_y + j, inner))).start())

        @pl.when(my_z != last)
        def _():
            piece_copy(mine + my_slot, grp, device(z, my_y)).start()

    def to_inner(piece):
        loop(1, inner, lambda j: piece_copy(piece, grp, device(my_z, lax.rem(my_y + j, inner))).start())

    def first_to_plane(z):
        def step(j):
            for g, w_ref in enumerate((wi_ref, wo_ref)):

                @pl.when(grp == g)
                def _(w_ref=w_ref):
                    pltpu.make_async_remote_copy(
                        src_ref=w_ref, dst_ref=wts.at[mine + my_slot], send_sem=ws_sem,
                        recv_sem=wr_sem.at[mine + my_slot],
                        device_id=to(device(z, lax.rem(my_y + j, inner))), device_id_type=MESH_ID,
                    ).start()

        loop(0, jnp.where(my_z == last, inner, 1), step)

    loop(0, jnp.minimum(my_z, 3), first_to_plane)

    loads[0].wait()
    loads[1].wait()
    xpad[0:half] = jnp.zeros((half, 8, channels), F32)
    xpad[axial + half : axial + 2 * half] = jnp.zeros((half, 8, channels), F32)

    def widen(i):
        for j in range(8):
            for r in range(2):
                xpad[half + i * 8 + j, 4 * r : 4 * r + 4, :] = xb[i * 8 + j, r].astype(F32)

    loop(0, axial // 8, widen)

    def exchange1(d):
        pltpu.make_async_remote_copy(
            src_ref=send1.at[d], dst_ref=recv1.at[me], send_sem=s1_sem, recv_sem=r1_sem.at[my_z],
            device_id=to(d), device_id_type=MESH_ID,
        ).start()

    def axial_chunk(i):
        acc = jnp.zeros((8, 8, channels), F32)
        for k in range(taps):
            acc = acc + xpad[pl.ds(i * 8 + k, 8)] * atv[k : k + 1, :][None]
        acc = acc.reshape(4, 2, 8, channels)
        low, high = swap_middle(acc[:, 0], acc[:, 1])
        send1[pl.ds(i * 4, 4)] = jnp.concatenate([low, high], axis=1).astype(BF16)
        loop(i * 4, jnp.minimum(i * 4 + 4, me), exchange1)

    loop(0, axial // 8, axial_chunk)

    for copy in loads[2:5]:
        copy.wait()
    unit = lax.broadcasted_iota(jnp.int32, (hl, channels), 0)
    lane = lax.broadcasted_iota(jnp.int32, (hl, channels), 1)
    place = (lane == unit + lax.rem(my_slot, per) * hl).astype(F32).astype(BF16)
    bias16 = jnp.broadcast_to(biv[...].astype(F32), (16, hl)).astype(BF16)
    bias[my_slot] = jnp.dot(bias16, place, preferred_element_type=F32)[0:1]

    def send_bias(d):
        pltpu.make_async_remote_copy(
            src_ref=bias.at[my_slot], dst_ref=bias.at[my_slot], send_sem=bs_sem, recv_sem=br_sem,
            device_id=to(d), device_id_type=MESH_ID,
        ).start()

    pltpu.make_async_copy(send1.at[me], recv1.at[me], r1_sem.at[my_z]).start()
    loop(3, my_z, to_plane)
    loop(0, me, send_bias)

    def upward(z):
        behind = jnp.where(z == my_z, lax.rem(me, q), -1)

        @pl.when(behind < q - 1)
        def _():
            pl.semaphore_wait(up_sem.at[z], q - 1 - behind)

        loop(z * q + behind + 1, z * q + q, exchange1)

        @pl.when(z == my_z)
        def _():
            to_inner(mine + my_slot)
            pl.when(my_z == last)(lambda: to_inner(theirs + my_slot))
            piece_copy(mine + my_slot, grp, sibling).start()
            piece_copy(theirs + my_slot, grp, sibling).start()

        @pl.when(z != my_z)
        def _():
            to_plane(z)

        loop(z * q + behind + 1, z * q + q, send_bias)

    loop(my_z, outer, upward)

    @pl.when(grp == 0)
    def _():
        pl.semaphore_wait(across_sem, 1)

    def pass_on(piece):
        piece_copy(piece, 1 - grp, me).start()
        piece_copy(piece, grp, sibling).start()

    def from_line(z):
        piece = mine + base + z * inner + my_y
        piece_copy(piece, grp, sibling).wait_recv()

        @pl.when(z != last)
        def _():
            to_inner(piece)

        pass_on(piece)

    def from_inner(z):
        def step(j):
            piece = mine + base + z * inner + lax.rem(my_y + j, inner)
            piece_copy(piece, grp, sibling).wait_recv()

            pl.when(inside)(lambda: piece_copy(piece, 1 - grp, me).start())
            piece_copy(piece, grp, sibling).start()

        loop(1, inner, step)

    def from_across(z, y):
        piece = theirs + base + z * inner + y
        piece_copy(piece, grp, sibling).wait_recv()

        piece_copy(piece, grp, sibling).start()


    def nearest(visit):
        def step(dist):
            for z in (my_z - dist, my_z + dist):

                @pl.when((z >= 0) & (z < outer))
                def _(z=z):
                    visit(z)

        loop(1, outer, step)

    @pl.when(inside)
    def _():
        from_inner(my_z)

    loop(0, my_z, lambda i: pl.when(inside | (i < 1))(lambda: from_line(my_z - 1 - i)))
    loop(my_z + 1, last, from_line)

    @pl.when(inside)
    def _():
        loop(1, inner, lambda j: piece_copy(theirs + my_slot, grp, device(last, lax.rem(my_y + j, inner))).start())

    pl.when(inside)(lambda: from_line(last))
    nearest(lambda z: pl.when(inside & (z == last))(lambda: from_inner(z)))

    rpad[0:half] = jnp.zeros((half, 8, channels), F32)
    rpad[2 * n + half : 2 * n + 2 * half] = jnp.zeros((half, 8, channels), F32)
    loads[5].wait()
    loads[6].wait()

    def take(z):
        plane = recv1.at[pl.ds(z * q, q)]
        pltpu.make_async_copy(plane, plane, r1_sem.at[z]).wait()
        v = recv1[z * q : z * q + q].astype(F32)
        rpad[half + 2 * z * q : half + 2 * z * q + 2 * q] = v.reshape(2 * q, 8, channels)

    my_half = lax.div(me, n // 2)

    def exchange2(d):
        @pl.when(d != me)
        def _():
            pltpu.make_async_remote_copy(
                src_ref=send2.at[d], dst_ref=recv2.at[me], send_sem=s2_sem, recv_sem=r2_sem.at[my_half],
                device_id=to(d), device_id_type=MESH_ID,
            ).start()

        @pl.when(d == me)
        def _():
            pltpu.make_async_copy(send2.at[me], recv2.at[me], r2_sem.at[my_half]).start()

    def radial_chunk(i):
        acc = jnp.zeros((8, 8, channels), F32)
        for k in range(taps):
            acc = acc + rpad[pl.ds(i * 8 + k, 8)] * rtv[k : k + 1, :][None]
        acc = acc + cbv[...][None]
        send2[pl.ds(i * 4, 4)] = acc.reshape(4, 16, channels).astype(BF16)
        loop(i * 4, i * 4 + 4, exchange2)

    taken = 0
    for z in range(outer):
        need = min(outer, (q * z + q - 1 + 8) // q + 1)
        for p in range(taken, need):
            take(p)
        taken = need
        loop(z * q // 4, (z + 1) * q // 4, radial_chunk)


    @pl.when(my_z == last)
    def _():
        from_inner(my_z)
        loop(0, my_z, lambda i: pl.when(jnp.logical_not((i < 1)))(lambda: from_line(my_z - 1 - i)))

    nearest(lambda z: pl.when(jnp.logical_not(inside & (z == last)))(lambda: from_inner(z)))

    def across_inner(j):
        y = lax.rem(my_y + j, inner)

        @pl.when(j > 0)
        def _():
            from_across(my_z, y)

        nearest(lambda z: from_across(z, y))

    loop(0, inner, across_inner)

    biases = bias.at[pl.ds(0, n - 1)]
    pltpu.make_async_copy(biases, biases, br_sem).wait()
    for copy in loads[7:]:
        copy.wait()
    block = min(16, n)
    rows = block * 16

    def norm(i):
        v = recv2[pl.ds(i * block, block)].reshape(rows, channels).astype(F32)
        average = jnp.mean(v, axis=-1, keepdims=True)
        centred = v - average
        variance = jnp.mean(centred * centred, axis=-1, keepdims=True)
        z = centred * lax.rsqrt(variance + 1e-06) * lgv[...] + lbv[...]
        normed[i] = z.astype(BF16)

    for h in range(2):
        part = recv2.at[pl.ds(0, n // 2)]
        pltpu.make_async_copy(part, part, r2_sem.at[h]).wait()
    loop(0, n // block, norm)

    def flat(w):
        if hl % 16:
            return w.astype(F32).reshape(per * hl, channels).astype(BF16)
        return w.reshape(per * hl, channels)

    def project(z, first):
        w_in = flat(wts[pl.ds(first, per)])
        w_out = flat(wts[pl.ds(n + first, per)])
        b_in = jnp.sum(bias[pl.ds(first, per)], axis=0)
        u = lax.dot_general(z, w_in, (((1,), (1,)), ((), ())), preferred_element_type=F32) + b_in
        g = 0.5 * u * (1.0 + jnp.tanh(0.7978845608028654 * (u + 0.044715 * (u * u * u))))
        return jnp.dot(g.astype(BF16), w_out, preferred_element_type=F32)

    def from_sibling(i):
        piece_copy(i, grp, sibling).wait_recv()
        piece_copy(n + i, grp, sibling).wait_recv()

    def half_mlp(first):
        def step(i):
            total = project(normed[i], first)
            for g in range(1, chips // per):
                total = total + project(normed[i], first + g * per)
            return total

        return step

    def own(i):
        sums[i] = half_mlp(base)(i)

    loop(0, n // block, own)
    loop(chips - base, n - base, from_sibling)

    def finish(i):
        total = sums[i] + half_mlp(chips - base)(i)
        branch = (lsv[...] * (total + bov[...])).astype(BF16).astype(F32)
        branch = branch.reshape(block, 2, 8, channels)
        for a, part in enumerate(swap_middle(branch[:, 0], branch[:, 1])):
            for s in range(block):
                at = 2 * (i * block + s) + a
                v = xpad[half + at] + part[s]
                for r in range(2):
                    o_ref[at, r] = v[4 * r : 4 * r + 4].astype(BF16)

    loop(0, n // block, finish)

    sent = send1.at[pl.ds(0, n - 1)]
    pltpu.make_async_copy(sent, sent, s1_sem).wait()
    sent2 = send2.at[pl.ds(0, n - 1)]
    pltpu.make_async_copy(sent2, sent2, s2_sem).wait()
    passed = wts.at[pl.ds(0, 2 * n - 2)]
    pltpu.make_async_copy(passed, passed, ws_sem).wait()
    pltpu.make_async_copy(biases, biases, bs_sem).wait()


def local(
    features,
    axial_taps,
    radial_taps,
    conv_bias,
    ln_gain,
    ln_bias,
    w_in,
    b_in,
    w_out,
    b_out,
    layer_scale,
    n,
    groups,
):
    axial, radial, theta, channels = features.shape
    taps = axial_taps.shape[0]
    hl = w_in.shape[0]
    inner = 1
    while 4 * inner * inner <= n // 2:
        inner *= 2
    assert groups == 2
    assert radial == 2 and theta == 4 and axial == 2 * n and channels == 256 and taps == 31

    def row(v):
        return v.reshape(1, -1)

    vmem = pl.BlockSpec(memory_space=pltpu.VMEM)
    hbm = pl.BlockSpec(memory_space=pltpu.HBM)
    dma = pltpu.SemaphoreType.DMA
    vec = pltpu.VMEM((1, channels), F32)
    return pl.pallas_call(
        functools.partial(kernel, n, inner, taps, hl),
        out_shape=pltpu.VMEM(features.shape, BF16),
        in_specs=[hbm] * 11,
        out_specs=vmem,
        scratch_shapes=[
            pltpu.VMEM(features.shape, BF16),
            pltpu.VMEM((taps, channels), F32),
            pltpu.VMEM((taps, channels), F32),
            vec, vec, vec,
            pltpu.VMEM((1, hl), BF16),
            vec, vec,
            pltpu.VMEM((axial + taps - 1, 8, channels), F32),
            pltpu.VMEM((2 * n + taps - 1, 8, channels), F32),
            pltpu.VMEM((n, 16, channels), BF16),
            pltpu.VMEM((n, 16, channels), BF16),
            pltpu.VMEM((n, 16, channels), BF16),
            pltpu.VMEM((n, 16, channels), BF16),
            pltpu.VMEM((2 * n, hl, channels), BF16),
            pltpu.VMEM((n, 1, channels), F32),
            pltpu.VMEM((n // min(16, n), 16 * min(16, n), channels), BF16),
            pltpu.VMEM((n // min(16, n), 16 * min(16, n), channels), F32),
            dma((11,)),
            pltpu.SemaphoreType.REGULAR((n // 2 // inner,)),
            pltpu.SemaphoreType.REGULAR,
            dma, dma((n // 2 // inner,)), dma, dma((2,)), dma,
            dma((2 * n,)), dma, dma,
        ],
        compiler_params=pltpu.CompilerParams(
            collective_id=0, has_side_effects=True, vmem_limit_bytes=60 * 1024 * 1024
        ),
        cost_estimate=pl.CostEstimate(
            flops=axial * 8 * channels * 4 * (n * hl + taps),
            bytes_accessed=4 * axial * 8 * channels + 4 * n * hl * channels,
            transcendentals=axial * 8 * n * hl,
        ),
    )(
        features, axial_taps, radial_taps, row(conv_bias), row(ln_gain), row(ln_bias),
        w_in, row(b_in), w_out, row(b_out), row(layer_scale),
    )


def solution(mesh):
    in_specs = (
        P("groups", "row", None, None),
        P(),
        P(),
        P(),
        P(),
        P(),
        P("row", None),
        P("row"),
        P("row", None),
        P(),
        P(),
    )
    out_specs = P("groups", "row", None, None)
    body = functools.partial(local, n=mesh.shape["row"], groups=mesh.shape["groups"])
    return jax.shard_map(body, mesh=mesh, in_specs=in_specs, out_specs=out_specs, check_vma=False)
```

```python
import functools

import jax
import jax.numpy as jnp
from jax import lax
from jax.experimental import pallas as pl
from jax.experimental.pallas import tpu as pltpu
from jax.sharding import PartitionSpec as P

MESH_ID = pl.DeviceIdType.MESH
F32 = jnp.float32
BF16 = jnp.bfloat16


def swap_middle(first, second):
    top = lax.broadcasted_iota(jnp.int32, first.shape, first.ndim - 2) < 4
    axis = first.ndim - 2
    return (
        jnp.where(top, first, pltpu.roll(second, 4, axis)),
        jnp.where(top, pltpu.roll(first, 4, axis), second),
    )


def kernel(
    n, inner, taps, hl,
    x_ref, at_ref, rt_ref, cb_ref, lg_ref, lb_ref, wi_ref, bi_ref, wo_ref, bo_ref, ls_ref,
    o_ref,
    xb, atv, rtv, cbv, lgv, lbv, biv, bov, lsv,
    xpad, rpad, send1, recv1, send2, recv2, wts, bias, normed, sums,
    in_sem, up_sem, across_sem, s1_sem, r1_sem, s2_sem, r2_sem, ws_sem, wr_sem, bs_sem, br_sem,
):
    channels = x_ref.shape[3]
    axial = x_ref.shape[0]
    half = taps // 2
    per = channels // hl
    chips = n // 2
    outer = chips // inner
    q = 2 * inner
    me = lax.axis_index("row")
    grp = lax.axis_index("groups")
    core = lax.rem(me, 2)
    my_chip = lax.div(me, 2)
    my_z = lax.div(my_chip, inner)
    my_y = lax.rem(my_chip, inner)
    sibling = me + 1 - 2 * core
    base = core * chips
    my_slot = base + my_chip
    last = outer - 1
    inside = my_z < last
    mine = grp * n
    theirs = (1 - grp) * n

    def to(d):
        return (grp, d)

    def loop(lo, hi, body):
        def step(i, c):
            body(i)
            return c

        lax.fori_loop(lo, hi, step, 0)

    barrier = pltpu.get_barrier_semaphore()
    loop(me + 1, n, lambda d: pl.semaphore_signal(barrier, inc=1, device_id=to(d), device_id_type=MESH_ID))

    @pl.when(grp == 0)
    def _():
        pl.semaphore_signal(barrier, inc=1, device_id=(1, me), device_id_type=MESH_ID)

    pairs = (
        (x_ref, xb), (at_ref, atv), (wi_ref, wts.at[my_slot]), (wo_ref, wts.at[n + my_slot]), (bi_ref, biv),
        (rt_ref, rtv), (cb_ref, cbv), (lg_ref, lgv), (lb_ref, lbv), (bo_ref, bov), (ls_ref, lsv),
    )
    loads = [pltpu.make_async_copy(a, b, in_sem.at[i]) for i, (a, b) in enumerate(pairs)]
    for copy in loads:
        copy.start()

    @pl.when(me + grp > 0)
    def _():
        pl.semaphore_wait(barrier, me + grp)

    @pl.when(grp == 1)
    def _():
        pl.semaphore_signal(across_sem, inc=1, device_id=(0, me), device_id_type=MESH_ID)

    loop(0, me, lambda d: pl.semaphore_signal(up_sem.at[my_z], inc=1, device_id=to(d), device_id_type=MESH_ID))

    def piece_copy(piece, g, d):
        return pltpu.make_async_remote_copy(
            src_ref=wts.at[piece], dst_ref=wts.at[piece], send_sem=ws_sem, recv_sem=wr_sem.at[piece],
            device_id=(g, d), device_id_type=MESH_ID,
        )

    def device(z, y):
        return 2 * (z * inner + y) + core

    def to_plane(z):
        @pl.when(my_z == last)
        def _():
            loop(0, inner, lambda j: piece_copy(mine + my_slot, grp, device(z, lax.rem(my_y + j, inner))).start())

        @pl.when(my_z != last)
        def _():
            piece_copy(mine + my_slot, grp, device(z, my_y)).start()

    def to_inner(piece):
        loop(1, inner, lambda j: piece_copy(piece, grp, device(my_z, lax.rem(my_y + j, inner))).start())

    def first_to_plane(z):
        def step(j):
            for g, w_ref in enumerate((wi_ref, wo_ref)):

                @pl.when(grp == g)
                def _(w_ref=w_ref):
                    pltpu.make_async_remote_copy(
                        src_ref=w_ref, dst_ref=wts.at[mine + my_slot], send_sem=ws_sem,
                        recv_sem=wr_sem.at[mine + my_slot],
                        device_id=to(device(z, lax.rem(my_y + j, inner))), device_id_type=MESH_ID,
                    ).start()

        loop(0, jnp.where(my_z == last, inner, 1), step)

    loop(0, jnp.minimum(my_z, 3), first_to_plane)

    loads[0].wait()
    loads[1].wait()
    xpad[0:half] = jnp.zeros((half, 8, channels), F32)
    xpad[axial + half : axial + 2 * half] = jnp.zeros((half, 8, channels), F32)

    def widen(i):
        for j in range(8):
            for r in range(2):
                xpad[half + i * 8 + j, 4 * r : 4 * r + 4, :] = xb[i * 8 + j, r].astype(F32)

    loop(0, axial // 8, widen)

    def exchange1(d):
        pltpu.make_async_remote_copy(
            src_ref=send1.at[d], dst_ref=recv1.at[me], send_sem=s1_sem, recv_sem=r1_sem.at[my_z],
            device_id=to(d), device_id_type=MESH_ID,
        ).start()

    def axial_chunk(i):
        acc = jnp.zeros((8, 8, channels), F32)
        for k in range(taps):
            acc = acc + xpad[pl.ds(i * 8 + k, 8)] * atv[k : k + 1, :][None]
        acc = acc.reshape(4, 2, 8, channels)
        low, high = swap_middle(acc[:, 0], acc[:, 1])
        send1[pl.ds(i * 4, 4)] = jnp.concatenate([low, high], axis=1).astype(BF16)
        loop(i * 4, jnp.minimum(i * 4 + 4, me), exchange1)

    loop(0, axial // 8, axial_chunk)

    for copy in loads[2:5]:
        copy.wait()
    unit = lax.broadcasted_iota(jnp.int32, (hl, channels), 0)
    lane = lax.broadcasted_iota(jnp.int32, (hl, channels), 1)
    place = (lane == unit + lax.rem(my_slot, per) * hl).astype(F32).astype(BF16)
    bias16 = jnp.broadcast_to(biv[...].astype(F32), (16, hl)).astype(BF16)
    bias[my_slot] = jnp.dot(bias16, place, preferred_element_type=F32)[0:1]

    def send_bias(d):
        pltpu.make_async_remote_copy(
            src_ref=bias.at[my_slot], dst_ref=bias.at[my_slot], send_sem=bs_sem, recv_sem=br_sem,
            device_id=to(d), device_id_type=MESH_ID,
        ).start()

    pltpu.make_async_copy(send1.at[me], recv1.at[me], r1_sem.at[my_z]).start()
    loop(3, my_z, to_plane)
    loop(0, me, send_bias)

    def upward(z):
        behind = jnp.where(z == my_z, lax.rem(me, q), -1)

        @pl.when(behind < q - 1)
        def _():
            pl.semaphore_wait(up_sem.at[z], q - 1 - behind)

        loop(z * q + behind + 1, z * q + q, exchange1)

        @pl.when(z == my_z)
        def _():
            to_inner(mine + my_slot)
            pl.when(my_z == last)(lambda: to_inner(theirs + my_slot))
            piece_copy(mine + my_slot, grp, sibling).start()
            piece_copy(theirs + my_slot, grp, sibling).start()

        @pl.when((z != my_z) & ((z < last) | (my_z == last - 1)))
        def _():
            to_plane(z)

        loop(z * q + behind + 1, z * q + q, send_bias)

    loop(my_z, last, upward)
    pl.when(jnp.logical_not(((my_z > 0) & (my_z < last - 1))))(lambda: upward(last))

    @pl.when(grp == 0)
    def _():
        pl.semaphore_wait(across_sem, 1)

    def pass_on(piece):
        piece_copy(piece, 1 - grp, me).start()
        piece_copy(piece, grp, sibling).start()

    def from_line(z):
        piece = mine + base + z * inner + my_y
        piece_copy(piece, grp, sibling).wait_recv()

        @pl.when(z != last)
        def _():
            to_inner(piece)

        pass_on(piece)

    def from_inner(z):
        def step(j):
            piece = mine + base + z * inner + lax.rem(my_y + j, inner)
            piece_copy(piece, grp, sibling).wait_recv()

            pl.when(inside)(lambda: piece_copy(piece, 1 - grp, me).start())
            piece_copy(piece, grp, sibling).start()

        loop(1, inner, step)

    def from_across(z, y):
        piece = theirs + base + z * inner + y
        piece_copy(piece, grp, sibling).wait_recv()

        piece_copy(piece, grp, sibling).start()


    def nearest(visit):
        def step(dist):
            for z in (my_z - dist, my_z + dist):

                @pl.when((z >= 0) & (z < outer))
                def _(z=z):
                    visit(z)

        loop(1, outer, step)

    @pl.when(inside)
    def _():
        from_inner(my_z)

    loop(0, my_z, lambda i: pl.when(inside | (i < 1))(lambda: from_line(my_z - 1 - i)))
    pl.when(((my_z > 0) & (my_z < last - 1)))(lambda: upward(last))
    loop(my_z + 1, last, from_line)
    pl.when(my_z < last - 1)(lambda: to_plane(last))

    @pl.when(inside)
    def _():
        loop(1, inner, lambda j: piece_copy(theirs + my_slot, grp, device(last, lax.rem(my_y + j, inner))).start())

    pl.when(inside)(lambda: from_line(last))
    nearest(lambda z: pl.when(inside & (z == last))(lambda: from_inner(z)))

    rpad[0:half] = jnp.zeros((half, 8, channels), F32)
    rpad[2 * n + half : 2 * n + 2 * half] = jnp.zeros((half, 8, channels), F32)
    loads[5].wait()
    loads[6].wait()

    def take(z):
        plane = recv1.at[pl.ds(z * q, q)]
        pltpu.make_async_copy(plane, plane, r1_sem.at[z]).wait()
        v = recv1[z * q : z * q + q].astype(F32)
        rpad[half + 2 * z * q : half + 2 * z * q + 2 * q] = v.reshape(2 * q, 8, channels)

    my_half = lax.div(me, n // 2)

    def exchange2(d):
        @pl.when(d != me)
        def _():
            pltpu.make_async_remote_copy(
                src_ref=send2.at[d], dst_ref=recv2.at[me], send_sem=s2_sem, recv_sem=r2_sem.at[my_half],
                device_id=to(d), device_id_type=MESH_ID,
            ).start()

        @pl.when(d == me)
        def _():
            pltpu.make_async_copy(send2.at[me], recv2.at[me], r2_sem.at[my_half]).start()

    def radial_chunk(i):
        acc = jnp.zeros((8, 8, channels), F32)
        for k in range(taps):
            acc = acc + rpad[pl.ds(i * 8 + k, 8)] * rtv[k : k + 1, :][None]
        acc = acc + cbv[...][None]
        send2[pl.ds(i * 4, 4)] = acc.reshape(4, 16, channels).astype(BF16)
        loop(i * 4, i * 4 + 4, exchange2)

    taken = 0
    for z in range(outer):
        need = min(outer, (q * z + q - 1 + 8) // q + 1)
        for p in range(taken, need):
            take(p)
        taken = need
        loop(z * q // 4, (z + 1) * q // 4, radial_chunk)


    @pl.when(my_z == last)
    def _():
        from_inner(my_z)
        loop(0, my_z, lambda i: pl.when(jnp.logical_not((i < 1)))(lambda: from_line(my_z - 1 - i)))

    nearest(lambda z: pl.when(jnp.logical_not(inside & (z == last)))(lambda: from_inner(z)))

    def across_inner(j):
        y = lax.rem(my_y + j, inner)

        @pl.when(j > 0)
        def _():
            from_across(my_z, y)

        nearest(lambda z: from_across(z, y))

    loop(0, inner, across_inner)

    biases = bias.at[pl.ds(0, n - 1)]
    pltpu.make_async_copy(biases, biases, br_sem).wait()
    for copy in loads[7:]:
        copy.wait()
    block = min(16, n)
    rows = block * 16

    def norm(i):
        v = recv2[pl.ds(i * block, block)].reshape(rows, channels).astype(F32)
        average = jnp.mean(v, axis=-1, keepdims=True)
        centred = v - average
        variance = jnp.mean(centred * centred, axis=-1, keepdims=True)
        z = centred * lax.rsqrt(variance + 1e-06) * lgv[...] + lbv[...]
        normed[i] = z.astype(BF16)

    for h in range(2):
        part = recv2.at[pl.ds(0, n // 2)]
        pltpu.make_async_copy(part, part, r2_sem.at[h]).wait()
    loop(0, n // block, norm)

    def flat(w):
        if hl % 16:
            return w.astype(F32).reshape(per * hl, channels).astype(BF16)
        return w.reshape(per * hl, channels)

    def project(z, first):
        w_in = flat(wts[pl.ds(first, per)])
        w_out = flat(wts[pl.ds(n + first, per)])
        b_in = jnp.sum(bias[pl.ds(first, per)], axis=0)
        u = lax.dot_general(z, w_in, (((1,), (1,)), ((), ())), preferred_element_type=F32) + b_in
        g = 0.5 * u * (1.0 + jnp.tanh(0.7978845608028654 * (u + 0.044715 * (u * u * u))))
        return jnp.dot(g.astype(BF16), w_out, preferred_element_type=F32)

    def from_sibling(i):
        piece_copy(i, grp, sibling).wait_recv()
        piece_copy(n + i, grp, sibling).wait_recv()

    def half_mlp(first):
        def step(i):
            total = project(normed[i], first)
            for g in range(1, chips // per):
                total = total + project(normed[i], first + g * per)
            return total

        return step

    def own(i):
        sums[i] = half_mlp(base)(i)

    loop(0, n // block, own)
    loop(chips - base, n - base, from_sibling)

    def finish(i):
        total = sums[i] + half_mlp(chips - base)(i)
        branch = (lsv[...] * (total + bov[...])).astype(BF16).astype(F32)
        branch = branch.reshape(block, 2, 8, channels)
        for a, part in enumerate(swap_middle(branch[:, 0], branch[:, 1])):
            for s in range(block):
                at = 2 * (i * block + s) + a
                v = xpad[half + at] + part[s]
                for r in range(2):
                    o_ref[at, r] = v[4 * r : 4 * r + 4].astype(BF16)

    loop(0, n // block, finish)

    sent = send1.at[pl.ds(0, n - 1)]
    pltpu.make_async_copy(sent, sent, s1_sem).wait()
    sent2 = send2.at[pl.ds(0, n - 1)]
    pltpu.make_async_copy(sent2, sent2, s2_sem).wait()
    passed = wts.at[pl.ds(0, 2 * n - 2)]
    pltpu.make_async_copy(passed, passed, ws_sem).wait()
    pltpu.make_async_copy(biases, biases, bs_sem).wait()


def local(
    features,
    axial_taps,
    radial_taps,
    conv_bias,
    ln_gain,
    ln_bias,
    w_in,
    b_in,
    w_out,
    b_out,
    layer_scale,
    n,
    groups,
):
    axial, radial, theta, channels = features.shape
    taps = axial_taps.shape[0]
    hl = w_in.shape[0]
    inner = 1
    while 4 * inner * inner <= n // 2:
        inner *= 2
    assert groups == 2
    assert radial == 2 and theta == 4 and axial == 2 * n and channels == 256 and taps == 31

    def row(v):
        return v.reshape(1, -1)

    vmem = pl.BlockSpec(memory_space=pltpu.VMEM)
    hbm = pl.BlockSpec(memory_space=pltpu.HBM)
    dma = pltpu.SemaphoreType.DMA
    vec = pltpu.VMEM((1, channels), F32)
    return pl.pallas_call(
        functools.partial(kernel, n, inner, taps, hl),
        out_shape=pltpu.VMEM(features.shape, BF16),
        in_specs=[hbm] * 11,
        out_specs=vmem,
        scratch_shapes=[
            pltpu.VMEM(features.shape, BF16),
            pltpu.VMEM((taps, channels), F32),
            pltpu.VMEM((taps, channels), F32),
            vec, vec, vec,
            pltpu.VMEM((1, hl), BF16),
            vec, vec,
            pltpu.VMEM((axial + taps - 1, 8, channels), F32),
            pltpu.VMEM((2 * n + taps - 1, 8, channels), F32),
            pltpu.VMEM((n, 16, channels), BF16),
            pltpu.VMEM((n, 16, channels), BF16),
            pltpu.VMEM((n, 16, channels), BF16),
            pltpu.VMEM((n, 16, channels), BF16),
            pltpu.VMEM((2 * n, hl, channels), BF16),
            pltpu.VMEM((n, 1, channels), F32),
            pltpu.VMEM((n // min(16, n), 16 * min(16, n), channels), BF16),
            pltpu.VMEM((n // min(16, n), 16 * min(16, n), channels), F32),
            dma((11,)),
            pltpu.SemaphoreType.REGULAR((n // 2 // inner,)),
            pltpu.SemaphoreType.REGULAR,
            dma, dma((n // 2 // inner,)), dma, dma((2,)), dma,
            dma((2 * n,)), dma, dma,
        ],
        compiler_params=pltpu.CompilerParams(
            collective_id=0, has_side_effects=True, vmem_limit_bytes=60 * 1024 * 1024
        ),
        cost_estimate=pl.CostEstimate(
            flops=axial * 8 * channels * 4 * (n * hl + taps),
            bytes_accessed=4 * axial * 8 * channels + 4 * n * hl * channels,
            transcendentals=axial * 8 * n * hl,
        ),
    )(
        features, axial_taps, radial_taps, row(conv_bias), row(ln_gain), row(ln_bias),
        w_in, row(b_in), w_out, row(b_out), row(layer_scale),
    )


def solution(mesh):
    in_specs = (
        P("groups", "row", None, None),
        P(),
        P(),
        P(),
        P(),
        P(),
        P("row", None),
        P("row"),
        P("row", None),
        P(),
        P(),
    )
    out_specs = P("groups", "row", None, None)
    body = functools.partial(local, n=mesh.shape["row"], groups=mesh.shape["groups"])
    return jax.shard_map(body, mesh=mesh, in_specs=in_specs, out_specs=out_specs, check_vma=False)
```

```python
import functools

import jax
import jax.numpy as jnp
from jax import lax
from jax.experimental import pallas as pl
from jax.experimental.pallas import tpu as pltpu
from jax.sharding import PartitionSpec as P

MESH_ID = pl.DeviceIdType.MESH
F32 = jnp.float32
BF16 = jnp.bfloat16


def swap_middle(first, second):
    top = lax.broadcasted_iota(jnp.int32, first.shape, first.ndim - 2) < 4
    axis = first.ndim - 2
    return (
        jnp.where(top, first, pltpu.roll(second, 4, axis)),
        jnp.where(top, pltpu.roll(first, 4, axis), second),
    )


def kernel(
    n, inner, taps, hl,
    x_ref, at_ref, rt_ref, cb_ref, lg_ref, lb_ref, wi_ref, bi_ref, wo_ref, bo_ref, ls_ref,
    o_ref,
    xb, atv, rtv, cbv, lgv, lbv, biv, bov, lsv,
    xpad, rpad, send1, recv1, send2, recv2, wts, bias, normed, sums,
    in_sem, up_sem, across_sem, s1_sem, r1_sem, s2_sem, r2_sem, ws_sem, wr_sem, bs_sem, br_sem,
):
    channels = x_ref.shape[3]
    axial = x_ref.shape[0]
    half = taps // 2
    per = channels // hl
    chips = n // 2
    outer = chips // inner
    q = 2 * inner
    me = lax.axis_index("row")
    grp = lax.axis_index("groups")
    core = lax.rem(me, 2)
    my_chip = lax.div(me, 2)
    my_z = lax.div(my_chip, inner)
    my_y = lax.rem(my_chip, inner)
    sibling = me + 1 - 2 * core
    base = core * chips
    my_slot = base + my_chip
    last = outer - 1
    inside = my_z < last
    mine = grp * n
    theirs = (1 - grp) * n

    def to(d):
        return (grp, d)

    def loop(lo, hi, body):
        def step(i, c):
            body(i)
            return c

        lax.fori_loop(lo, hi, step, 0)

    barrier = pltpu.get_barrier_semaphore()
    loop(me + 1, n, lambda d: pl.semaphore_signal(barrier, inc=1, device_id=to(d), device_id_type=MESH_ID))

    @pl.when(grp == 0)
    def _():
        pl.semaphore_signal(barrier, inc=1, device_id=(1, me), device_id_type=MESH_ID)

    pairs = (
        (x_ref, xb), (at_ref, atv), (wi_ref, wts.at[my_slot]), (wo_ref, wts.at[n + my_slot]), (bi_ref, biv),
        (rt_ref, rtv), (cb_ref, cbv), (lg_ref, lgv), (lb_ref, lbv), (bo_ref, bov), (ls_ref, lsv),
    )
    loads = [pltpu.make_async_copy(a, b, in_sem.at[i]) for i, (a, b) in enumerate(pairs)]
    for copy in loads:
        copy.start()

    @pl.when(me + grp > 0)
    def _():
        pl.semaphore_wait(barrier, me + grp)

    @pl.when(grp == 1)
    def _():
        pl.semaphore_signal(across_sem, inc=1, device_id=(0, me), device_id_type=MESH_ID)

    loop(0, me, lambda d: pl.semaphore_signal(up_sem.at[my_z], inc=1, device_id=to(d), device_id_type=MESH_ID))

    def piece_copy(piece, g, d):
        return pltpu.make_async_remote_copy(
            src_ref=wts.at[piece], dst_ref=wts.at[piece], send_sem=ws_sem, recv_sem=wr_sem.at[piece],
            device_id=(g, d), device_id_type=MESH_ID,
        )

    def device(z, y):
        return 2 * (z * inner + y) + core

    def to_plane(z):
        @pl.when(my_z == last)
        def _():
            loop(0, inner, lambda j: piece_copy(mine + my_slot, grp, device(z, lax.rem(my_y + j, inner))).start())

        @pl.when(my_z != last)
        def _():
            piece_copy(mine + my_slot, grp, device(z, my_y)).start()

    def to_inner(piece):
        loop(1, inner, lambda j: piece_copy(piece, grp, device(my_z, lax.rem(my_y + j, inner))).start())

    def first_to_plane(z):
        def step(j):
            for g, w_ref in enumerate((wi_ref, wo_ref)):

                @pl.when(grp == g)
                def _(w_ref=w_ref):
                    pltpu.make_async_remote_copy(
                        src_ref=w_ref, dst_ref=wts.at[mine + my_slot], send_sem=ws_sem,
                        recv_sem=wr_sem.at[mine + my_slot],
                        device_id=to(device(z, lax.rem(my_y + j, inner))), device_id_type=MESH_ID,
                    ).start()

        loop(0, jnp.where(my_z == last, inner, 1), step)

    loop(0, jnp.minimum(my_z, 3), first_to_plane)

    loads[0].wait()
    loads[1].wait()
    xpad[0:half] = jnp.zeros((half, 8, channels), F32)
    xpad[axial + half : axial + 2 * half] = jnp.zeros((half, 8, channels), F32)

    def widen(i):
        for j in range(8):
            for r in range(2):
                xpad[half + i * 8 + j, 4 * r : 4 * r + 4, :] = xb[i * 8 + j, r].astype(F32)

    loop(0, axial // 8, widen)

    def exchange1(d):
        pltpu.make_async_remote_copy(
            src_ref=send1.at[d], dst_ref=recv1.at[me], send_sem=s1_sem, recv_sem=r1_sem.at[my_z],
            device_id=to(d), device_id_type=MESH_ID,
        ).start()

    def axial_chunk(i):
        acc = jnp.zeros((8, 8, channels), F32)
        for k in range(taps):
            acc = acc + xpad[pl.ds(i * 8 + k, 8)] * atv[k : k + 1, :][None]
        acc = acc.reshape(4, 2, 8, channels)
        low, high = swap_middle(acc[:, 0], acc[:, 1])
        send1[pl.ds(i * 4, 4)] = jnp.concatenate([low, high], axis=1).astype(BF16)
        loop(i * 4, jnp.minimum(i * 4 + 4, me), exchange1)

    loop(0, axial // 8, axial_chunk)

    for copy in loads[2:5]:
        copy.wait()
    unit = lax.broadcasted_iota(jnp.int32, (hl, channels), 0)
    lane = lax.broadcasted_iota(jnp.int32, (hl, channels), 1)
    place = (lane == unit + lax.rem(my_slot, per) * hl).astype(F32).astype(BF16)
    bias16 = jnp.broadcast_to(biv[...].astype(F32), (16, hl)).astype(BF16)
    bias[my_slot] = jnp.dot(bias16, place, preferred_element_type=F32)[0:1]

    def send_bias(d):
        pltpu.make_async_remote_copy(
            src_ref=bias.at[my_slot], dst_ref=bias.at[my_slot], send_sem=bs_sem, recv_sem=br_sem,
            device_id=to(d), device_id_type=MESH_ID,
        ).start()

    pltpu.make_async_copy(send1.at[me], recv1.at[me], r1_sem.at[my_z]).start()
    loop(3, my_z, to_plane)

    def upward(z):
        behind = jnp.where(z == my_z, lax.rem(me, q), -1)

        @pl.when(behind < q - 1)
        def _():
            pl.semaphore_wait(up_sem.at[z], q - 1 - behind)

        loop(z * q + behind + 1, z * q + q, exchange1)

        @pl.when(z == my_z)
        def _():
            to_inner(mine + my_slot)
            pl.when(my_z == last)(lambda: to_inner(theirs + my_slot))
            piece_copy(mine + my_slot, grp, sibling).start()
            piece_copy(theirs + my_slot, grp, sibling).start()

        @pl.when((z != my_z) & ((z < last) | (my_z == last - 1)))
        def _():
            to_plane(z)

        loop(z * q + behind + 1, z * q + q, send_bias)

    loop(my_z, last, upward)
    loop(0, me, send_bias)
    pl.when(jnp.logical_not(((my_z > 0) & (my_z < last - 1))))(lambda: upward(last))

    @pl.when(grp == 0)
    def _():
        pl.semaphore_wait(across_sem, 1)

    def pass_on(piece):
        piece_copy(piece, 1 - grp, me).start()
        piece_copy(piece, grp, sibling).start()

    def from_line(z):
        piece = mine + base + z * inner + my_y
        piece_copy(piece, grp, sibling).wait_recv()

        @pl.when(z != last)
        def _():
            to_inner(piece)

        pass_on(piece)

    def from_inner(z):
        def step(j):
            piece = mine + base + z * inner + lax.rem(my_y + j, inner)
            piece_copy(piece, grp, sibling).wait_recv()

            pl.when(inside)(lambda: piece_copy(piece, 1 - grp, me).start())
            piece_copy(piece, grp, sibling).start()

        loop(1, inner, step)

    def from_across(z, y):
        piece = theirs + base + z * inner + y
        piece_copy(piece, grp, sibling).wait_recv()

        piece_copy(piece, grp, sibling).start()


    def nearest(visit):
        def step(dist):
            for z in (my_z - dist, my_z + dist):

                @pl.when((z >= 0) & (z < outer))
                def _(z=z):
                    visit(z)

        loop(1, outer, step)

    @pl.when(inside)
    def _():
        from_inner(my_z)

    loop(0, my_z, lambda i: pl.when(inside | (i < 1))(lambda: from_line(my_z - 1 - i)))
    pl.when(((my_z > 0) & (my_z < last - 1)))(lambda: upward(last))
    loop(my_z + 1, last, from_line)
    pl.when(my_z < last - 1)(lambda: to_plane(last))

    @pl.when(inside)
    def _():
        loop(1, inner, lambda j: piece_copy(theirs + my_slot, grp, device(last, lax.rem(my_y + j, inner))).start())

    pl.when(inside)(lambda: from_line(last))
    nearest(lambda z: pl.when(inside & (z == last))(lambda: from_inner(z)))

    rpad[0:half] = jnp.zeros((half, 8, channels), F32)
    rpad[2 * n + half : 2 * n + 2 * half] = jnp.zeros((half, 8, channels), F32)
    loads[5].wait()
    loads[6].wait()

    def take(z):
        plane = recv1.at[pl.ds(z * q, q)]
        pltpu.make_async_copy(plane, plane, r1_sem.at[z]).wait()
        v = recv1[z * q : z * q + q].astype(F32)
        rpad[half + 2 * z * q : half + 2 * z * q + 2 * q] = v.reshape(2 * q, 8, channels)

    my_half = lax.div(me, n // 2)

    def exchange2(d):
        @pl.when(d != me)
        def _():
            pltpu.make_async_remote_copy(
                src_ref=send2.at[d], dst_ref=recv2.at[me], send_sem=s2_sem, recv_sem=r2_sem.at[my_half],
                device_id=to(d), device_id_type=MESH_ID,
            ).start()

        @pl.when(d == me)
        def _():
            pltpu.make_async_copy(send2.at[me], recv2.at[me], r2_sem.at[my_half]).start()

    def radial_chunk(i):
        acc = jnp.zeros((8, 8, channels), F32)
        for k in range(taps):
            acc = acc + rpad[pl.ds(i * 8 + k, 8)] * rtv[k : k + 1, :][None]
        acc = acc + cbv[...][None]
        send2[pl.ds(i * 4, 4)] = acc.reshape(4, 16, channels).astype(BF16)
        loop(i * 4, i * 4 + 4, exchange2)

    taken = 0
    for z in range(outer):
        need = min(outer, (q * z + q - 1 + 8) // q + 1)
        for p in range(taken, need):
            take(p)
        taken = need
        loop(z * q // 4, (z + 1) * q // 4, radial_chunk)


    @pl.when(my_z == last)
    def _():
        from_inner(my_z)
        loop(0, my_z, lambda i: pl.when(jnp.logical_not((i < 1)))(lambda: from_line(my_z - 1 - i)))

    nearest(lambda z: pl.when(jnp.logical_not(inside & (z == last)))(lambda: from_inner(z)))

    def across_inner(j):
        y = lax.rem(my_y + j, inner)

        @pl.when(j > 0)
        def _():
            from_across(my_z, y)

        nearest(lambda z: from_across(z, y))

    loop(0, inner, across_inner)

    biases = bias.at[pl.ds(0, n - 1)]
    pltpu.make_async_copy(biases, biases, br_sem).wait()
    for copy in loads[7:]:
        copy.wait()
    block = min(16, n)
    rows = block * 16

    def norm(i):
        v = recv2[pl.ds(i * block, block)].reshape(rows, channels).astype(F32)
        average = jnp.mean(v, axis=-1, keepdims=True)
        centred = v - average
        variance = jnp.mean(centred * centred, axis=-1, keepdims=True)
        z = centred * lax.rsqrt(variance + 1e-06) * lgv[...] + lbv[...]
        normed[i] = z.astype(BF16)

    for h in range(2):
        part = recv2.at[pl.ds(0, n // 2)]
        pltpu.make_async_copy(part, part, r2_sem.at[h]).wait()
    loop(0, n // block, norm)

    def flat(w):
        if hl % 16:
            return w.astype(F32).reshape(per * hl, channels).astype(BF16)
        return w.reshape(per * hl, channels)

    def project(z, first):
        w_in = flat(wts[pl.ds(first, per)])
        w_out = flat(wts[pl.ds(n + first, per)])
        b_in = jnp.sum(bias[pl.ds(first, per)], axis=0)
        u = lax.dot_general(z, w_in, (((1,), (1,)), ((), ())), preferred_element_type=F32) + b_in
        g = 0.5 * u * (1.0 + jnp.tanh(0.7978845608028654 * (u + 0.044715 * (u * u * u))))
        return jnp.dot(g.astype(BF16), w_out, preferred_element_type=F32)

    def from_sibling(i):
        piece_copy(i, grp, sibling).wait_recv()
        piece_copy(n + i, grp, sibling).wait_recv()

    def half_mlp(first):
        def step(i):
            total = project(normed[i], first)
            for g in range(1, chips // per):
                total = total + project(normed[i], first + g * per)
            return total

        return step

    def own(i):
        sums[i] = half_mlp(base)(i)

    loop(0, n // block, own)
    loop(chips - base, n - base, from_sibling)

    def finish(i):
        total = sums[i] + half_mlp(chips - base)(i)
        branch = (lsv[...] * (total + bov[...])).astype(BF16).astype(F32)
        branch = branch.reshape(block, 2, 8, channels)
        for a, part in enumerate(swap_middle(branch[:, 0], branch[:, 1])):
            for s in range(block):
                at = 2 * (i * block + s) + a
                v = xpad[half + at] + part[s]
                for r in range(2):
                    o_ref[at, r] = v[4 * r : 4 * r + 4].astype(BF16)

    loop(0, n // block, finish)

    sent = send1.at[pl.ds(0, n - 1)]
    pltpu.make_async_copy(sent, sent, s1_sem).wait()
    sent2 = send2.at[pl.ds(0, n - 1)]
    pltpu.make_async_copy(sent2, sent2, s2_sem).wait()
    passed = wts.at[pl.ds(0, 2 * n - 2)]
    pltpu.make_async_copy(passed, passed, ws_sem).wait()
    pltpu.make_async_copy(biases, biases, bs_sem).wait()


def local(
    features,
    axial_taps,
    radial_taps,
    conv_bias,
    ln_gain,
    ln_bias,
    w_in,
    b_in,
    w_out,
    b_out,
    layer_scale,
    n,
    groups,
):
    axial, radial, theta, channels = features.shape
    taps = axial_taps.shape[0]
    hl = w_in.shape[0]
    inner = 1
    while 4 * inner * inner <= n // 2:
        inner *= 2
    assert groups == 2
    assert radial == 2 and theta == 4 and axial == 2 * n and channels == 256 and taps == 31

    def row(v):
        return v.reshape(1, -1)

    vmem = pl.BlockSpec(memory_space=pltpu.VMEM)
    hbm = pl.BlockSpec(memory_space=pltpu.HBM)
    dma = pltpu.SemaphoreType.DMA
    vec = pltpu.VMEM((1, channels), F32)
    return pl.pallas_call(
        functools.partial(kernel, n, inner, taps, hl),
        out_shape=pltpu.VMEM(features.shape, BF16),
        in_specs=[hbm] * 11,
        out_specs=vmem,
        scratch_shapes=[
            pltpu.VMEM(features.shape, BF16),
            pltpu.VMEM((taps, channels), F32),
            pltpu.VMEM((taps, channels), F32),
            vec, vec, vec,
            pltpu.VMEM((1, hl), BF16),
            vec, vec,
            pltpu.VMEM((axial + taps - 1, 8, channels), F32),
            pltpu.VMEM((2 * n + taps - 1, 8, channels), F32),
            pltpu.VMEM((n, 16, channels), BF16),
            pltpu.VMEM((n, 16, channels), BF16),
            pltpu.VMEM((n, 16, channels), BF16),
            pltpu.VMEM((n, 16, channels), BF16),
            pltpu.VMEM((2 * n, hl, channels), BF16),
            pltpu.VMEM((n, 1, channels), F32),
            pltpu.VMEM((n // min(16, n), 16 * min(16, n), channels), BF16),
            pltpu.VMEM((n // min(16, n), 16 * min(16, n), channels), F32),
            dma((11,)),
            pltpu.SemaphoreType.REGULAR((n // 2 // inner,)),
            pltpu.SemaphoreType.REGULAR,
            dma, dma((n // 2 // inner,)), dma, dma((2,)), dma,
            dma((2 * n,)), dma, dma,
        ],
        compiler_params=pltpu.CompilerParams(
            collective_id=0, has_side_effects=True, vmem_limit_bytes=60 * 1024 * 1024
        ),
        cost_estimate=pl.CostEstimate(
            flops=axial * 8 * channels * 4 * (n * hl + taps),
            bytes_accessed=4 * axial * 8 * channels + 4 * n * hl * channels,
            transcendentals=axial * 8 * n * hl,
        ),
    )(
        features, axial_taps, radial_taps, row(conv_bias), row(ln_gain), row(ln_bias),
        w_in, row(b_in), w_out, row(b_out), row(layer_scale),
    )


def solution(mesh):
    in_specs = (
        P("groups", "row", None, None),
        P(),
        P(),
        P(),
        P(),
        P(),
        P("row", None),
        P("row"),
        P("row", None),
        P(),
        P(),
    )
    out_specs = P("groups", "row", None, None)
    body = functools.partial(local, n=mesh.shape["row"], groups=mesh.shape["groups"])
    return jax.shard_map(body, mesh=mesh, in_specs=in_specs, out_specs=out_specs, check_vma=False)
```
